512 devices in a mesh: wide: 128 (over x, y, z_hi, core), chan: 4 (over z_lo).
Axes of the slice: x: 4, y: 4, z: 16 (z_hi: 4, z_lo: 4; z = z_hi * 4 + z_lo), core: 2. Of those that a mesh axis runs over, the one named last changes fastest.
Arguments:
- activations: bfloat16 [8192, 53248], P(('wide', 'chan')), may hold values from -6 to 6
- grads: bfloat16 [8192, 16384], P(('wide', 'chan')), may hold values from -15 to 15
Outputs:
- gram: float32 [4, 256, 53248], P('chan', None, 'wide')
The draws below stay inside these ranges and needn't reach their ends.
All inputs are finite; a program needn't handle non-finite values.
Results may differ from the reference program's by a relative error of at most 0.004.
Values may be sent and summed in bfloat16 or wider, within the bound.
A program may use at most 64 MiB of HBM per device.

```python
import math
import jax
import jax.numpy as jnp
from jax import lax

DIN = 53248
DOUT = 16384
GROUPS = 4
ROWS = 256
TOKENS = 8192


def draw_grads(key, part):
    key = jax.random.fold_in(key, 11)
    key_scale, key_value = jax.random.split(key)
    logs = jax.random.uniform(key_scale, (TOKENS, GROUPS), jnp.float32, math.log(0.3), math.log(3.0))
    values = jnp.clip(jax.random.normal(key_value, (TOKENS, DOUT), jnp.float32), -5.0, 5.0)
    scales = jnp.repeat(jnp.exp(logs), DOUT // GROUPS, axis=1)
    return (values * scales).astype(jnp.bfloat16)


def level_of(key, dims, shards, least, high):
    gain = 1.0
    for dim, shards_of in shards:
        steps = jax.random.uniform(jax.random.fold_in(jax.random.fold_in(key, 6), dim), (shards_of,), jnp.float32, least / len(shards), high / len(shards))
        gain = gain * jnp.repeat(jnp.exp(steps), dims[dim] // shards_of).reshape((-1,) + (1,) * (len(dims) - 1 - dim))
    return gain


def centred(rng, dims, spread, bound, cuts=(), held_as=jnp.bfloat16):
    entries = spread * jax.random.normal(rng, dims, jnp.float32)
    if cuts:
        entries = entries * level_of(rng, dims, cuts, -0.22, 0.18)
    return jnp.clip(entries, -bound, bound).astype(held_as)


def setup_inputs(seed: int = 0) -> dict:
    key_of = jax.random.split(jax.random.key(seed), 3)
    return {
        "activations": centred(key_of[0], (TOKENS, DIN), 1.0, 6.0, ((0, 512),)),
        "grads": draw_grads(jax.random.fold_in(key_of[2], 71), 0),
    }


def reference(activations, grads):
    per_group = DOUT // GROUPS
    squares = grads.astype(jnp.float32) ** 2
    fisher = lax.optimization_barrier(jnp.mean(squares.reshape(TOKENS, GROUPS, per_group), axis=2)).astype(jnp.bfloat16)
    window = activations[:, :ROWS].astype(jnp.float32)
    factor = 1.0 / math.sqrt(TOKENS)

    def one_group(column):
        weighted = (column.astype(jnp.float32)[:, None] * window).astype(jnp.bfloat16)
        product = lax.dot_general(weighted, activations, (((0,), (0,)), ((), ())), preferred_element_type=jnp.float32)
        return product * factor
    return lax.map(one_group, fisher.T)
```

```python
import functools
import math

import jax
import jax.numpy as jnp
from jax import lax
from jax.experimental import pallas as pl
from jax.experimental.pallas import tpu as pltpu
from jax.sharding import PartitionSpec as P

MESH = pl.DeviceIdType.MESH
ROWS = 256
HALF = ROWS // 2
LANES = 128
SPAN = 4
TILE = 416
FULL = TILE // LANES
REST = TILE - FULL * LANES
PACK = LANES // REST
CHUNK = FULL * HALF + HALF // PACK


def quarter_order(group_len):
    ring = SPAN * group_len
    half = ring // 2
    first = [half] * SPAN
    for spot in range(group_len):
        order = [2, 1, 3, 0] if 2 * spot < group_len else [2, 3, 1, 0]
        for step in range(half):
            far = half - step
            for place in (spot + far, spot - far):
                slot = order.index((place // group_len) % SPAN)
                first[slot] = min(first[slot], step)
    first[3] = min(first[3], half)
    return first


def kernel(
    peers, group_len, factor,
    act, grads, out,
    gbuf, stage, win, raw, wt, prod, acc, sbuf, rbuf,
    load_sem, win_send, win_recv, raw_send, raw_recv, ring_send, ring_recv,
):
    wide = lax.axis_index("wide")
    chan = lax.axis_index("chan")
    tok = act.shape[0]
    ring = SPAN * group_len
    half = ring // 2
    core = lax.rem(wide, 2)
    run = lax.rem(lax.div(wide, 2), SPAN)
    line = lax.div(wide, 2 * SPAN)
    me = line * 2 + core
    place = run * group_len + chan

    def plane_device(peer):
        return (lax.div(peer, 2) * (2 * SPAN) + run * 2 + lax.rem(peer, 2), chan)

    def ring_device(spot):
        return (line * (2 * SPAN) + lax.div(spot, group_len) * 2 + core, lax.rem(spot, group_len))

    after = ring_device(lax.rem(place + 1, ring))
    before = ring_device(lax.rem(place + ring - 1, ring))

    barrier = pltpu.get_barrier_semaphore()

    def greet(step, carry):
        peer = lax.rem(me + step, peers)
        pl.semaphore_signal(barrier, inc=1, device_id=plane_device(peer), device_id_type=MESH)
        return carry

    load_grads = pltpu.make_async_copy(grads, gbuf, load_sem.at[0])
    load_grads.start()
    load_win = pltpu.make_async_copy(act.at[:, pl.ds(0, ROWS)], stage.at[:, pl.ds(0, ROWS)], load_sem.at[1])
    load_win.start()
    for neighbour in (after, before):
        pl.semaphore_signal(barrier, inc=1, device_id=neighbour, device_id_type=MESH)
    lax.fori_loop(1, peers, greet, 0)

    load_grads.wait()
    per_group = grads.shape[1] // group_len
    lane = lax.broadcasted_iota(jnp.int32, (tok, LANES), 1)
    weights = jnp.zeros((tok, LANES), jnp.float32)
    for group in range(group_len):
        part = gbuf[:, group * per_group : (group + 1) * per_group].astype(jnp.float32)
        mean = jnp.sum(part * part, axis=1, keepdims=True) * (1.0 / per_group)
        weights = jnp.where(lane == group, mean, weights)
    stage[:, ROWS : ROWS + LANES] = weights.astype(jnp.bfloat16)
    load_win.wait()

    pl.semaphore_wait(barrier, peers + 1)

    mine = pl.ds(pl.multiple_of(me * tok, tok), tok)

    def send_win(step, carry):
        peer = lax.rem(me + step, peers)
        pltpu.make_async_remote_copy(
            src_ref=stage, dst_ref=win.at[mine], send_sem=win_send, recv_sem=win_recv,
            device_id=plane_device(peer), device_id_type=MESH,
        ).start()
        return carry

    pltpu.make_async_copy(stage, win.at[mine], win_recv).start()
    lax.fori_loop(1, peers, send_win, 0)

    early = 2 * chan < group_len
    quarters = [
        lax.rem(run + 2, SPAN),
        lax.rem(run + jnp.where(early, 1, 3), SPAN),
        lax.rem(run + jnp.where(early, 3, 1), SPAN),
        run,
    ]

    def columns(peer, quarter):
        tile = 2 * quarter + lax.rem(peer, 2)
        block = lax.div(peer, 2) * (2 * SPAN * TILE // LANES) + FULL * tile + lax.div(tile, PACK)
        return pl.ds(pl.multiple_of(block * LANES, LANES), (FULL + 1) * LANES)

    def send_raw(slot):
        def send(step, carry):
            peer = lax.rem(me + step, peers)
            pltpu.make_async_remote_copy(
                src_ref=act.at[:, columns(peer, quarters[slot])], dst_ref=raw.at[slot, mine],
                send_sem=raw_send.at[slot], recv_sem=raw_recv.at[slot],
                device_id=plane_device(peer), device_id_type=MESH,
            ).start()
            return carry

        pltpu.make_async_copy(
            act.at[:, columns(me, quarters[slot])], raw.at[slot, mine], raw_recv.at[slot]
        ).start()
        lax.fori_loop(1, peers, send, 0)

    for slot in range(SPAN):
        send_raw(slot)

    pltpu.make_async_copy(win, win, win_recv).wait()
    turned = jnp.transpose(win[:, :ROWS].astype(jnp.float32))
    turned_weights = jnp.transpose(win[:, ROWS : ROWS + LANES].astype(jnp.float32))
    for group in range(group_len):
        wt[group] = (turned_weights[group : group + 1, :] * turned).astype(jnp.bfloat16)

    def multiply(slot):
        quarter = quarters[slot]
        skew = lax.rem(2 * quarter + core, PACK) * REST
        pltpu.make_async_copy(raw.at[slot], raw.at[slot], raw_recv.at[slot]).wait()
        place_in = lax.broadcasted_iota(jnp.int32, (HALF, LANES), 1)
        keep = place_in < LANES - skew

        def one_group(group, carry):
            prod[...] = jnp.dot(wt[group], raw[slot], preferred_element_type=jnp.float32)
            for part in range(2):
                rows = pl.ds(part * HALF, HALF)
                back = lax.rem(LANES - skew, LANES)
                turned_blocks = [
                    pltpu.roll(prod[rows, pl.ds(j * LANES, LANES)], back, 1) for j in range(FULL + 1)
                ]
                for j in range(FULL):
                    acc[quarter, group, part, pl.ds(j * HALF, HALF), :] = jnp.where(
                        keep, turned_blocks[j], turned_blocks[j + 1]
                    )
                few = HALF // PACK
                which = lax.div(lax.broadcasted_iota(jnp.int32, (few, LANES), 1), REST)
                rest = jnp.zeros((few, LANES), jnp.float32)
                for j in range(PACK):
                    piece = prod[pl.ds(part * HALF + j * few, few), pl.ds(FULL * LANES, LANES)]
                    piece = pltpu.roll(piece, lax.rem(LANES - skew + j * REST, LANES), 1)
                    rest = jnp.where(which == j, piece, rest)
                acc[quarter, group, part, pl.ds(FULL * HALF, few), :] = rest
            return carry

        lax.fori_loop(0, group_len, one_group, 0)

    need = quarter_order(group_len)

    def ring_copy(way, step, part):
        return pltpu.make_async_remote_copy(
            src_ref=sbuf.at[way, step, part], dst_ref=rbuf.at[way, step, part],
            send_sem=ring_send.at[way, step, part], recv_sem=ring_recv.at[way, step, part],
            device_id=after if way == 0 else before, device_id_type=MESH,
        )

    sent = []
    for step in range(half):
        for slot in range(SPAN):
            if need[slot] == step:
                multiply(slot)
        far = half - step
        for part in range(2):
            for way in range(2):
                if step == 0 and way != part:
                    continue
                goal = lax.rem(place + far if way == 0 else place + ring - far, ring)
                total = acc[lax.div(goal, group_len), lax.rem(goal, group_len), part]
                if step > 1 or (step == 1 and way == part):
                    ring_copy(way, step - 1, part).wait_recv()
                    total = total + rbuf[way, step - 1, part].astype(jnp.float32)
                sbuf[way, step, part] = total.astype(jnp.bfloat16)
                copy = ring_copy(way, step, part)
                copy.start()
                sent.append(copy)
    for slot in range(SPAN):
        if need[slot] == half:
            multiply(slot)

    for part in range(2):
        total = acc[run, chan, part]
        for way in range(2):
            ring_copy(way, half - 1, part).wait_recv()
            total = total + rbuf[way, half - 1, part].astype(jnp.float32)
        total = total * factor
        for j in range(FULL):
            out[0, pl.ds(part * HALF, HALF), pl.ds(j * LANES, LANES)] = total[j * HALF : (j + 1) * HALF]
        few = HALF // PACK
        rest = total[FULL * HALF :]
        for j in range(PACK):
            piece = pltpu.roll(rest, (LANES - j * REST) % LANES, 1)
            out[0, pl.ds(part * HALF + j * few, few), pl.ds(FULL * LANES, REST)] = piece[:, :REST]

    for copy in sent:
        copy.wait_send()
    others = pl.ds(0, (peers - 1) * tok)
    pltpu.make_async_copy(win.at[others], win.at[others], win_send).wait()
    for slot in range(SPAN):
        pltpu.make_async_copy(raw.at[slot, others], raw.at[slot, others], raw_send.at[slot]).wait()


def solution(mesh):
    wide, group_len = mesh.shape["wide"], mesh.shape["chan"]
    peers = wide // SPAN
    half = SPAN * group_len // 2

    def step(activations, grads):
        tok = activations.shape[0]
        plane = peers * tok
        factor = 1.0 / math.sqrt(plane * SPAN * group_len)
        return pl.pallas_call(
            functools.partial(kernel, peers, group_len, factor),
            out_shape=jax.ShapeDtypeStruct((1, ROWS, TILE), jnp.float32),
            in_specs=[pl.BlockSpec(memory_space=pl.ANY)] * 2,
            out_specs=pl.BlockSpec(memory_space=pltpu.VMEM),
            scratch_shapes=[
                pltpu.VMEM(grads.shape, jnp.bfloat16),
                pltpu.VMEM((tok, ROWS + LANES), jnp.bfloat16),
                pltpu.VMEM((plane, ROWS + LANES), jnp.bfloat16),
                pltpu.VMEM((SPAN, plane, (FULL + 1) * LANES), jnp.bfloat16),
                pltpu.VMEM((group_len, ROWS, plane), jnp.bfloat16),
                pltpu.VMEM((ROWS, (FULL + 1) * LANES), jnp.float32),
                pltpu.VMEM((SPAN, group_len, 2, CHUNK, LANES), jnp.float32),
                pltpu.VMEM((2, half, 2, CHUNK, LANES), jnp.bfloat16),
                pltpu.VMEM((2, half, 2, CHUNK, LANES), jnp.bfloat16),
                pltpu.SemaphoreType.DMA((2,)),
                pltpu.SemaphoreType.DMA,
                pltpu.SemaphoreType.DMA,
                pltpu.SemaphoreType.DMA((SPAN,)),
                pltpu.SemaphoreType.DMA((SPAN,)),
                pltpu.SemaphoreType.DMA((2, half, 2)),
                pltpu.SemaphoreType.DMA((2, half, 2)),
            ],
            compiler_params=pltpu.CompilerParams(
                collective_id=0, has_side_effects=True, vmem_limit_bytes=48 * 1024 * 1024
            ),
        )(activations, grads)

    return jax.shard_map(
        step,
        mesh=mesh,
        in_specs=(P(("wide", "chan"), None), P(("wide", "chan"), None)),
        out_specs=P("chan", None, "wide"),
        check_vma=False,
    )
```

```python
import functools
import math

import jax
import jax.numpy as jnp
from jax import lax
from jax.experimental import pallas as pl
from jax.experimental.pallas import tpu as pltpu
from jax.sharding import PartitionSpec as P

MESH = pl.DeviceIdType.MESH
ROWS = 256
LANES = 128
SPAN = 4
TILE = 416
FULL = TILE // LANES
MAIN = FULL * LANES
REST = TILE - MAIN
PACK = LANES // REST
FEW = ROWS // PACK
BLOCK = MAIN // LANES * ROWS + FEW
PARTS = 2
PART = ROWS // PARTS
CHUNK = FULL * PART
WHERE = [pl.ds(part * CHUNK, CHUNK) for part in range(PARTS)] + [pl.ds(PARTS * CHUNK, FEW)]
LAST = PARTS
AT = [[0, 1, 2], [3, 4, 5], [6, 7, 8], [10, 11, 12]]
AT_LAST = 9
MESSAGES = [(0, 3), (3, 3), (6, 4), (10, 3)]
BLOCKS = 13
LINE = 2 * SPAN * TILE // LANES
WIDTH = 4
STRIDE = 5


def first_steps(group_len):
    ring = SPAN * group_len
    half = ring // 2
    table = []
    for spot in range(group_len):
        order = [2, 1, 3, 0] if 2 * spot < group_len else [2, 3, 1, 0]
        first = [half] * SPAN
        for step in range(half):
            far = half - step
            for place in (spot + far, spot - far):
                slot = order.index((place // group_len) % SPAN)
                first[slot] = min(first[slot], step)
        table.append(first)
    return table


def kernel(
    peers, group_len, factor,
    act_hbm, grads_hbm, out,
    gbuf, act, head, packed, win, raw, wt, own, own_last, sbuf, rbuf,
    load_sem, win_send, win_recv, raw_send, raw_recv, ring_send, ring_recv,
):
    wide = lax.axis_index("wide")
    chan = lax.axis_index("chan")
    tok = act.shape[0]
    ring = SPAN * group_len
    half = ring // 2
    lines = peers // 2
    rows_y = 4 if lines % 4 == 0 else 1
    rows_x = lines // rows_y
    core = lax.rem(wide, 2)
    run = lax.rem(lax.div(wide, 2), SPAN)
    line = lax.div(wide, 2 * SPAN)
    me = line * 2 + core
    lead = core * lines + line
    place = run * group_len + chan
    width = min(WIDTH, peers)

    def plane_device(spot, side):
        return (spot * (2 * SPAN) + run * 2 + side, chan)

    def ring_device(spot):
        return (line * (2 * SPAN) + lax.div(spot, group_len) * 2 + core, lax.rem(spot, group_len))

    all_x = [lax.rem(lax.div(line, rows_y) + step, rows_x) for step in range(rows_x)]
    all_y = [lax.rem(line + step, rows_y) for step in range(rows_y)]
    other_lines = []
    for step in range(1, lines):
        step = step * STRIDE % lines
        other_lines.append(all_x[step // rows_y] * rows_y + all_y[step % rows_y])
    twin = 1 - core
    peer_list = [(spot, side) for spot in other_lines for side in (core, twin)] + [(line, twin)]

    after = ring_device(lax.rem(place + 1, ring))
    before = ring_device(lax.rem(place + ring - 1, ring))

    barrier = pltpu.get_barrier_semaphore()

    load_grads = pltpu.make_async_copy(grads_hbm, gbuf, load_sem.at[0])
    load_grads.start()
    load_act = pltpu.make_async_copy(act_hbm, act, load_sem.at[1])
    load_act.start()
    for neighbour in (after, before):
        pl.semaphore_signal(barrier, inc=1, device_id=neighbour, device_id_type=MESH)
    for spot, side in peer_list:
        pl.semaphore_signal(barrier, inc=1, device_id=plane_device(spot, side), device_id_type=MESH)

    load_grads.wait()
    per_group = gbuf.shape[1] // group_len
    lane = lax.broadcasted_iota(jnp.int32, (tok, LANES), 1)
    weights = jnp.zeros((tok, LANES), jnp.float32)
    for group in range(group_len):
        part = gbuf[:, group * per_group : (group + 1) * per_group].astype(jnp.float32)
        mean = jnp.sum(part * part, axis=1, keepdims=True) * (1.0 / per_group)
        weights = jnp.where(lane == group, mean, weights)
    weights = weights.astype(jnp.bfloat16)
    load_act.wait()
    head[:, :ROWS] = act[:, :ROWS]
    head[:, ROWS:] = weights

    early = 2 * chan < group_len
    quarters = [
        lax.rem(run + 2, SPAN),
        lax.rem(run + jnp.where(early, 1, 3), SPAN),
        lax.rem(run + jnp.where(early, 3, 1), SPAN),
        run,
    ]

    def slot_of(quarter):
        ahead = lax.rem(quarter + SPAN - run, SPAN)
        one = jnp.where(early, 1, 2)
        return jnp.where(ahead == 2, 0, jnp.where(ahead == 0, 3, jnp.where(ahead == 1, one, 3 - one)))

    def block_of(peer, quarter):
        tile = 2 * quarter + lax.rem(peer, 2)
        block = lax.div(peer, 2) * LINE + FULL * tile + lax.div(tile, PACK)
        return block, lax.rem(tile, PACK) * REST

    def lanes(block):
        return pl.ds(pl.multiple_of(block * LANES, LANES), LANES)

    def turn(value, shift):
        return pltpu.roll(value, lax.rem(shift + LANES, LANES), 1)

    def fill(message):
        first, count = MESSAGES[message]

        def some(group, carry):
            for number in range(width):
                peer = group * width + number
                for slot in range(SPAN):
                    wanted = [j for j in range(FULL) if first <= AT[slot][j] < first + count]
                    if not wanted:
                        continue
                    block, skew = block_of(peer, quarters[slot])
                    turned = {
                        j: turn(act[:, lanes(block + j)], -skew) for j in range(wanted[0], wanted[-1] + 2)
                    }
                    for j in wanted:
                        packed[peer, :, AT[slot][j] * LANES : (AT[slot][j] + 1) * LANES] = jnp.where(
                            lane < LANES - skew, turned[j], turned[j + 1]
                        )
                if first <= AT_LAST < first + count:
                    rest = jnp.zeros((tok, LANES), jnp.bfloat16)
                    for slot in range(SPAN):
                        block, skew = block_of(peer, quarters[slot])
                        piece = turn(act[:, lanes(block + FULL)], slot * REST - skew)
                        rest = jnp.where(lax.div(lane, REST) == slot, piece, rest)
                    packed[peer, :, AT_LAST * LANES : (AT_LAST + 1) * LANES] = rest
            return carry

        lax.fori_loop(0, peers // width, some, 0)

    fill(0)

    pl.semaphore_wait(barrier, peers + 1)

    mine = pl.ds(pl.multiple_of(lead * tok, tok), tok)
    side_rows = pl.ds(pl.multiple_of(core * lines * tok, tok), lines * tok)
    twin_rows = pl.ds(pl.multiple_of(twin * lines * tok, tok), lines * tok)

    def send_head():
        pltpu.make_async_copy(head, win.at[mine], win_recv.at[0]).start()
        for spot in other_lines:
            pltpu.make_async_remote_copy(
                src_ref=head, dst_ref=win.at[mine], send_sem=win_send.at[0], recv_sem=win_recv.at[0],
                device_id=plane_device(spot, core), device_id_type=MESH,
            ).start()

    def size_of(message):
        first, count = MESSAGES[message]
        return pl.ds(first * LANES, count * LANES)

    def send_raw(message):
        size = size_of(message)
        pltpu.make_async_copy(packed.at[me, :, size], raw.at[mine, size], raw_recv.at[message]).start()
        for spot, side in peer_list:
            pltpu.make_async_remote_copy(
                src_ref=packed.at[spot * 2 + side, :, size], dst_ref=raw.at[mine, size],
                send_sem=raw_send.at[message], recv_sem=raw_recv.at[message],
                device_id=plane_device(spot, side), device_id_type=MESH,
            ).start()

    def take_raw(message):
        all_of = raw.at[:, size_of(message)]
        pltpu.make_async_copy(all_of, all_of, raw_recv.at[message]).wait()

    send_head()
    send_raw(0)
    pltpu.make_async_copy(win.at[side_rows], win.at[side_rows], win_recv.at[0]).wait()
    hand_over = pltpu.make_async_remote_copy(
        src_ref=win.at[side_rows], dst_ref=win.at[side_rows], send_sem=win_send.at[1], recv_sem=win_recv.at[1],
        device_id=plane_device(line, twin), device_id_type=MESH,
    )
    hand_over.start()
    fill(1)
    send_raw(1)
    fill(2)
    fill(3)

    pltpu.make_async_copy(win.at[twin_rows], win.at[twin_rows], win_recv.at[1]).wait()

    turned_rows = jnp.transpose(win[:, :ROWS].astype(jnp.float32))
    turned_weights = jnp.transpose(win[:, ROWS : ROWS + LANES].astype(jnp.float32))
    for group in range(group_len):
        wt[group] = (turned_weights[group : group + 1, :] * turned_rows).astype(jnp.bfloat16)

    table = first_steps(group_len)
    third = min(table[spot][2] for spot in range(group_len))

    def take_at(step):
        for slot in range(SPAN):
            spots = [spot for spot in range(group_len) if table[spot][slot] == step]
            if slot == 2:
                spots = list(range(group_len)) if step == third else []
            if len(spots) == group_len:
                take_raw(slot)
            elif spots:
                hit = chan == spots[0]
                for spot in spots[1:]:
                    hit = jnp.logical_or(hit, chan == spot)
                pl.when(hit)(functools.partial(take_raw, slot))

    few_lane = lax.div(lax.broadcasted_iota(jnp.int32, (FEW, LANES), 1), REST)

    def choose(slot, values):
        picked = values[-1]
        for number in range(SPAN - 1):
            picked = jnp.where(slot == number, values[number], picked)
        return picked

    def multiply(way, step, goal, first, count):
        slot = slot_of(lax.div(goal, group_len))
        start = pl.multiple_of(choose(slot, [AT[number][first] for number in range(SPAN)]) * LANES, LANES)
        main = jnp.dot(
            wt[lax.rem(goal, group_len)], raw[:, pl.ds(start, count * LANES)], preferred_element_type=jnp.float32
        )
        for part in range(PARTS):
            for j in range(count):
                top = part * CHUNK + (first + j) * PART
                own[way, step, top : top + PART] = main[
                    part * PART : (part + 1) * PART, j * LANES : (j + 1) * LANES
                ]

    def multiply_last():
        for group in range(group_len):
            last = jnp.dot(
                wt[group], raw[:, AT_LAST * LANES : (AT_LAST + 1) * LANES], preferred_element_type=jnp.float32
            )
            for slot in range(SPAN):
                rest = jnp.zeros((FEW, LANES), jnp.float32)
                for j in range(PACK):
                    piece = last[j * FEW : (j + 1) * FEW]
                    shift = (j - slot) % PACK * REST
                    rest = jnp.where(few_lane == j, pltpu.roll(piece, shift, 1) if shift else piece, rest)
                own_last[slot, group] = rest

    def ring_copy(way, step, part):
        return pltpu.make_async_remote_copy(
            src_ref=sbuf.at[way, step, WHERE[part]], dst_ref=rbuf.at[way, step, WHERE[part]],
            send_sem=ring_send.at[way, step, part], recv_sem=ring_recv.at[way, step, part],
            device_id=after if way == 0 else before, device_id_type=MESH,
        )

    parts = list(range(PARTS))
    opening = [parts[: PARTS // 2], parts[PARTS // 2 :] + [LAST]]
    orders = [parts[PARTS // 2 :] + parts[: PARTS // 2], parts]

    def goal_of(way, step):
        far = half - step
        return lax.rem(place + far if way == 0 else place + ring - far, ring)

    def own_part(way, step, part, goal):
        if part == LAST:
            return own_last[slot_of(lax.div(goal, group_len)), lax.rem(goal, group_len)]
        return own[way, step, WHERE[part]]

    sent = []

    def pass_on(step, last):
        for number in range(1 if last else PARTS):
            for way in range(2):
                part = LAST if last else orders[way][number]
                if step == 0 and part not in opening[way]:
                    continue
                total = own_part(way if step else 0, step, part, goal_of(way, step))
                if step > 1 or (step == 1 and part in opening[way]):
                    ring_copy(way, step - 1, part).wait_recv()
                    total = total + rbuf[way, step - 1, WHERE[part]].astype(jnp.float32)
                sbuf[way, step, WHERE[part]] = total.astype(jnp.bfloat16)
                copy = ring_copy(way, step, part)
                copy.start()
                sent.append(copy)

    def prepare(step, first, count):
        if step == half:
            multiply(1, 0, place, first, count)
            return
        for way in range(1 if step == 0 else 2):
            multiply(way, step, goal_of(way, step), first, count)

    done = 0
    for step in range(half + 1):
        take_at(step)
        prepare(step, 0, FULL)
        if step == half:
            break
        if step == third:
            multiply_last()
        for late in range(2):
            if step >= third and done <= step:
                pass_on(done, True)
                done += 1
            if late == 0:
                pass_on(step, False)
        if step < 2:
            send_raw(2 + step)
    while done < half:
        pass_on(done, True)
        done += 1

    for part in parts + [LAST]:
        total = own_part(1, 0, part, place)
        for way in range(2):
            ring_copy(way, half - 1, part).wait_recv()
            total = total + rbuf[way, half - 1, WHERE[part]].astype(jnp.float32)
        total = jnp.transpose(total * factor)
        if part == LAST:
            for j in range(PACK):
                out[0, MAIN:TILE, j * FEW : (j + 1) * FEW] = total[j * REST : (j + 1) * REST]
        else:
            for j in range(FULL):
                out[0, j * LANES : (j + 1) * LANES, part * PART : (part + 1) * PART] = total[
                    :, j * PART : (j + 1) * PART
                ]

    for copy in sent:
        copy.wait_send()
    others = pl.ds(0, (peers - 1) * tok)
    hand_over.wait_send()
    half_others = pl.ds(0, (lines - 1) * tok)
    if lines > 1:
        pltpu.make_async_copy(win.at[half_others], win.at[half_others], win_send.at[0]).wait()
    for message in range(len(MESSAGES)):
        sent_of = raw.at[others, size_of(message)]
        pltpu.make_async_copy(sent_of, sent_of, raw_send.at[message]).wait()


def solution(mesh):
    wide, group_len = mesh.shape["wide"], mesh.shape["chan"]
    peers = wide // SPAN
    half = SPAN * group_len // 2

    def step(activations, grads):
        tok = activations.shape[0]
        plane = peers * tok
        factor = 1.0 / math.sqrt(plane * SPAN * group_len)
        gram = pl.pallas_call(
            functools.partial(kernel, peers, group_len, factor),
            out_shape=jax.ShapeDtypeStruct((1, TILE, ROWS), jnp.float32),
            in_specs=[pl.BlockSpec(memory_space=pltpu.HBM)] * 2,
            out_specs=pl.BlockSpec(memory_space=pltpu.VMEM),
            scratch_shapes=[
                pltpu.VMEM(grads.shape, jnp.bfloat16),
                pltpu.VMEM(activations.shape, jnp.bfloat16),
                pltpu.VMEM((tok, ROWS + LANES), jnp.bfloat16),
                pltpu.VMEM((peers, tok, BLOCKS * LANES), jnp.bfloat16),
                pltpu.VMEM((plane, ROWS + LANES), jnp.bfloat16),
                pltpu.VMEM((plane, BLOCKS * LANES), jnp.bfloat16),
                pltpu.VMEM((group_len, ROWS, plane), jnp.bfloat16),
                pltpu.VMEM((2, half, BLOCK, LANES), jnp.float32),
                pltpu.VMEM((SPAN, group_len, FEW, LANES), jnp.float32),
                pltpu.VMEM((2, half, BLOCK, LANES), jnp.bfloat16),
                pltpu.VMEM((2, half, BLOCK, LANES), jnp.bfloat16),
                pltpu.SemaphoreType.DMA((2,)),
                pltpu.SemaphoreType.DMA((2,)),
                pltpu.SemaphoreType.DMA((2,)),
                pltpu.SemaphoreType.DMA((len(MESSAGES),)),
                pltpu.SemaphoreType.DMA((len(MESSAGES),)),
                pltpu.SemaphoreType.DMA((2, half, LAST + 1)),
                pltpu.SemaphoreType.DMA((2, half, LAST + 1)),
            ],
            compiler_params=pltpu.CompilerParams(
                collective_id=0, has_side_effects=True, vmem_limit_bytes=62 * 1024 * 1024
            ),
        )(activations, grads)
        return jnp.transpose(gram, (0, 2, 1))

    return jax.shard_map(
        step,
        mesh=mesh,
        in_specs=(P(("wide", "chan"), None), P(("wide", "chan"), None)),
        out_specs=P("chan", None, "wide"),
        check_vma=False,
    )
```

```python
import functools
import math

import jax
import jax.numpy as jnp
from jax import lax
from jax.experimental import pallas as pl
from jax.experimental.pallas import tpu as pltpu
from jax.sharding import PartitionSpec as P

MESH = pl.DeviceIdType.MESH
ROWS = 256
LANES = 128
SPAN = 4
TILE = 416
FULL = TILE // LANES
MAIN = FULL * LANES
REST = TILE - MAIN
PACK = LANES // REST
FEW = ROWS // PACK
BLOCK = MAIN // LANES * ROWS + FEW
HALF = ROWS // 2
WHERE = [pl.ds(part * HALF, HALF) for part in range(2 * FULL)] + [pl.ds(FULL * ROWS, FEW)]
LAST = 2 * FULL
AT = [[0, 2, 3], [1, 4, 5], [6, 7, 8], [10, 11, 12]]
AT_LAST = 9
MESSAGES = [(0, 2), (2, 2), (4, 2), (6, 4), (10, 3)]
BLOCKS = 13
LINE = 2 * SPAN * TILE // LANES
WIDTH = 4
STRIDE = 5


def first_steps(group_len):
    ring = SPAN * group_len
    half = ring // 2
    table = []
    for spot in range(group_len):
        order = [2, 1, 3, 0] if 2 * spot < group_len else [2, 3, 1, 0]
        first = [half] * SPAN
        for step in range(half):
            far = half - step
            for place in (spot + far, spot - far):
                slot = order.index((place // group_len) % SPAN)
                first[slot] = min(first[slot], step)
        table.append(first)
    return table


def kernel(
    peers, group_len, factor,
    act_hbm, grads_hbm, out,
    gbuf, act, head, packed, win, raw, wt, own, own_last, sbuf, rbuf,
    load_sem, win_send, win_recv, raw_send, raw_recv, ring_send, ring_recv,
):
    wide = lax.axis_index("wide")
    chan = lax.axis_index("chan")
    tok = act.shape[0]
    ring = SPAN * group_len
    half = ring // 2
    lines = peers // 2
    rows_y = 4 if lines % 4 == 0 else 1
    rows_x = lines // rows_y
    core = lax.rem(wide, 2)
    run = lax.rem(lax.div(wide, 2), SPAN)
    line = lax.div(wide, 2 * SPAN)
    me = line * 2 + core
    lead = core * lines + line
    place = run * group_len + chan
    width = min(WIDTH, peers)

    def plane_device(spot, side):
        return (spot * (2 * SPAN) + run * 2 + side, chan)

    def ring_device(spot):
        return (line * (2 * SPAN) + lax.div(spot, group_len) * 2 + core, lax.rem(spot, group_len))

    all_x = [lax.rem(lax.div(line, rows_y) + step, rows_x) for step in range(rows_x)]
    all_y = [lax.rem(line + step, rows_y) for step in range(rows_y)]
    other_lines = []
    for step in range(1, lines):
        step = step * STRIDE % lines
        other_lines.append(all_x[step // rows_y] * rows_y + all_y[step % rows_y])
    twin = 1 - core
    peer_list = [(spot, side) for spot in other_lines for side in (core, twin)] + [(line, twin)]

    after = ring_device(lax.rem(place + 1, ring))
    before = ring_device(lax.rem(place + ring - 1, ring))

    barrier = pltpu.get_barrier_semaphore()

    load_grads = pltpu.make_async_copy(grads_hbm, gbuf, load_sem.at[0])
    load_grads.start()
    load_act = pltpu.make_async_copy(act_hbm, act, load_sem.at[1])
    load_act.start()
    for neighbour in (after, before):
        pl.semaphore_signal(barrier, inc=1, device_id=neighbour, device_id_type=MESH)
    for spot, side in peer_list:
        pl.semaphore_signal(barrier, inc=1, device_id=plane_device(spot, side), device_id_type=MESH)

    load_grads.wait()
    per_group = gbuf.shape[1] // group_len
    lane = lax.broadcasted_iota(jnp.int32, (tok, LANES), 1)
    weights = jnp.zeros((tok, LANES), jnp.float32)
    for group in range(group_len):
        part = gbuf[:, group * per_group : (group + 1) * per_group].astype(jnp.float32)
        mean = jnp.sum(part * part, axis=1, keepdims=True) * (1.0 / per_group)
        weights = jnp.where(lane == group, mean, weights)
    weights = weights.astype(jnp.bfloat16)
    load_act.wait()
    head[:, :ROWS] = act[:, :ROWS]
    head[:, ROWS:] = weights

    early = 2 * chan < group_len
    quarters = [
        lax.rem(run + 2, SPAN),
        lax.rem(run + jnp.where(early, 1, 3), SPAN),
        lax.rem(run + jnp.where(early, 3, 1), SPAN),
        run,
    ]

    def slot_of(quarter):
        ahead = lax.rem(quarter + SPAN - run, SPAN)
        one = jnp.where(early, 1, 2)
        return jnp.where(ahead == 2, 0, jnp.where(ahead == 0, 3, jnp.where(ahead == 1, one, 3 - one)))

    def block_of(peer, quarter):
        tile = 2 * quarter + lax.rem(peer, 2)
        block = lax.div(peer, 2) * LINE + FULL * tile + lax.div(tile, PACK)
        return block, lax.rem(tile, PACK) * REST

    def lanes(block):
        return pl.ds(pl.multiple_of(block * LANES, LANES), LANES)

    def turn(value, shift):
        return pltpu.roll(value, lax.rem(shift + LANES, LANES), 1)

    def fill(message):
        first, count = MESSAGES[message]

        def some(group, carry):
            for number in range(width):
                peer = group * width + number
                for slot in range(SPAN):
                    wanted = [j for j in range(FULL) if first <= AT[slot][j] < first + count]
                    if not wanted:
                        continue
                    block, skew = block_of(peer, quarters[slot])
                    turned = {
                        j: turn(act[:, lanes(block + j)], -skew) for j in range(wanted[0], wanted[-1] + 2)
                    }
                    for j in wanted:
                        packed[peer, :, AT[slot][j] * LANES : (AT[slot][j] + 1) * LANES] = jnp.where(
                            lane < LANES - skew, turned[j], turned[j + 1]
                        )
                if first <= AT_LAST < first + count:
                    rest = jnp.zeros((tok, LANES), jnp.bfloat16)
                    for slot in range(SPAN):
                        block, skew = block_of(peer, quarters[slot])
                        piece = turn(act[:, lanes(block + FULL)], slot * REST - skew)
                        rest = jnp.where(lax.div(lane, REST) == slot, piece, rest)
                    packed[peer, :, AT_LAST * LANES : (AT_LAST + 1) * LANES] = rest
            return carry

        lax.fori_loop(0, peers // width, some, 0)

    fill(0)

    pl.semaphore_wait(barrier, peers + 1)

    mine = pl.ds(pl.multiple_of(lead * tok, tok), tok)
    side_rows = pl.ds(pl.multiple_of(core * lines * tok, tok), lines * tok)
    twin_rows = pl.ds(pl.multiple_of(twin * lines * tok, tok), lines * tok)

    def send_head():
        pltpu.make_async_copy(head, win.at[mine], win_recv.at[0]).start()
        for spot in other_lines:
            pltpu.make_async_remote_copy(
                src_ref=head, dst_ref=win.at[mine], send_sem=win_send.at[0], recv_sem=win_recv.at[0],
                device_id=plane_device(spot, core), device_id_type=MESH,
            ).start()

    def size_of(message):
        first, count = MESSAGES[message]
        return pl.ds(first * LANES, count * LANES)

    def send_raw(message):
        size = size_of(message)
        pltpu.make_async_copy(packed.at[me, :, size], raw.at[mine, size], raw_recv.at[message]).start()
        for spot, side in peer_list:
            pltpu.make_async_remote_copy(
                src_ref=packed.at[spot * 2 + side, :, size], dst_ref=raw.at[mine, size],
                send_sem=raw_send.at[message], recv_sem=raw_recv.at[message],
                device_id=plane_device(spot, side), device_id_type=MESH,
            ).start()

    def take_raw(message):
        all_of = raw.at[:, size_of(message)]
        pltpu.make_async_copy(all_of, all_of, raw_recv.at[message]).wait()

    send_head()
    send_raw(0)
    for message in (1, 2):
        fill(message)
        send_raw(message)
    pltpu.make_async_copy(win.at[side_rows], win.at[side_rows], win_recv.at[0]).wait()
    hand_over = pltpu.make_async_remote_copy(
        src_ref=win.at[side_rows], dst_ref=win.at[side_rows], send_sem=win_send.at[1], recv_sem=win_recv.at[1],
        device_id=plane_device(line, twin), device_id_type=MESH,
    )
    hand_over.start()
    fill(3)
    fill(4)

    pltpu.make_async_copy(win.at[twin_rows], win.at[twin_rows], win_recv.at[1]).wait()

    turned_rows = jnp.transpose(win[:, :ROWS].astype(jnp.float32))
    turned_weights = jnp.transpose(win[:, ROWS : ROWS + LANES].astype(jnp.float32))
    for group in range(group_len):
        wt[group] = (turned_weights[group : group + 1, :] * turned_rows).astype(jnp.bfloat16)

    table = first_steps(group_len)
    third = min(table[spot][2] for spot in range(group_len))

    def take_fourth(step):
        spots = [spot for spot in range(group_len) if table[spot][3] == step]
        if not spots:
            return
        hit = chan == spots[0]
        for spot in spots[1:]:
            hit = jnp.logical_or(hit, chan == spot)
        pl.when(hit)(lambda: take_raw(4))

    few_lane = lax.div(lax.broadcasted_iota(jnp.int32, (FEW, LANES), 1), REST)

    def choose(slot, values):
        picked = values[-1]
        for number in range(SPAN - 1):
            picked = jnp.where(slot == number, values[number], picked)
        return picked

    def multiply(way, step, goal, first, count):
        slot = slot_of(lax.div(goal, group_len))
        start = pl.multiple_of(choose(slot, [AT[number][first] for number in range(SPAN)]) * LANES, LANES)
        main = jnp.dot(
            wt[lax.rem(goal, group_len)], raw[:, pl.ds(start, count * LANES)], preferred_element_type=jnp.float32
        )
        for j in range(count):
            own[way, step, (first + j) * ROWS : (first + j + 1) * ROWS] = main[:, j * LANES : (j + 1) * LANES]

    def multiply_last():
        for group in range(group_len):
            last = jnp.dot(
                wt[group], raw[:, AT_LAST * LANES : (AT_LAST + 1) * LANES], preferred_element_type=jnp.float32
            )
            for slot in range(SPAN):
                rest = jnp.zeros((FEW, LANES), jnp.float32)
                for j in range(PACK):
                    piece = last[j * FEW : (j + 1) * FEW]
                    shift = (j - slot) % PACK * REST
                    rest = jnp.where(few_lane == j, pltpu.roll(piece, shift, 1) if shift else piece, rest)
                own_last[slot, group] = rest

    def ring_copy(way, step, part):
        return pltpu.make_async_remote_copy(
            src_ref=sbuf.at[way, step, WHERE[part]], dst_ref=rbuf.at[way, step, WHERE[part]],
            send_sem=ring_send.at[way, step, part], recv_sem=ring_recv.at[way, step, part],
            device_id=after if way == 0 else before, device_id_type=MESH,
        )

    opening = [[0, 2, 4], [1, 3, 5, LAST]]

    def goal_of(way, step):
        far = half - step
        return lax.rem(place + far if way == 0 else place + ring - far, ring)

    def own_part(way, step, part, goal):
        if part == LAST:
            return own_last[slot_of(lax.div(goal, group_len)), lax.rem(goal, group_len)]
        return own[way, step, WHERE[part]]

    sent = []

    def pass_on(step, blocks):
        for block in blocks:
            pair = [LAST] if block == FULL else [2 * block, 2 * block + 1]
            for number in range(len(pair)):
                for way in range(2):
                    part = pair[number if way else len(pair) - 1 - number]
                    if step == 0 and part not in opening[way]:
                        continue
                    total = own_part(way if step else 0, step, part, goal_of(way, step))
                    if step > 1 or (step == 1 and part in opening[way]):
                        ring_copy(way, step - 1, part).wait_recv()
                        total = total + rbuf[way, step - 1, WHERE[part]].astype(jnp.float32)
                    sbuf[way, step, WHERE[part]] = total.astype(jnp.bfloat16)
                    copy = ring_copy(way, step, part)
                    copy.start()
                    sent.append(copy)

    def prepare(step, first, count):
        if step == half:
            multiply(1, 0, place, first, count)
            return
        for way in range(1 if step == 0 else 2):
            multiply(way, step, goal_of(way, step), first, count)

    take_raw(0)
    prepare(0, 0, 1)
    pass_on(0, [0])
    prepare(1, 0, 1)
    pass_on(1, [0])
    take_raw(1)
    prepare(0, 1, 2)
    pass_on(0, [1, 2])
    send_raw(3)
    take_raw(2)
    prepare(1, 1, 2)
    pass_on(1, [1, 2])
    send_raw(4)
    done = 0
    taken = False
    for step in range(2, half + 1):
        if step >= third and not taken:
            take_raw(3)
            taken = True
            multiply_last()
            for earlier in range(step):
                take_fourth(earlier)
        take_fourth(step)
        prepare(step, 0, 1)
        prepare(step, 1, 2)
        if step == half:
            break
        if taken and done <= step:
            pass_on(done, [FULL])
            done += 1
        pass_on(step, [0, 1, 2])
        if taken and done <= step:
            pass_on(done, [FULL])
            done += 1
    while done < half:
        pass_on(done, [FULL])
        done += 1

    for block in range(FULL + 1):
        for part in [LAST] if block == FULL else [2 * block, 2 * block + 1]:
            total = own_part(1, 0, part, place)
            for way in range(2):
                ring_copy(way, half - 1, part).wait_recv()
                total = total + rbuf[way, half - 1, WHERE[part]].astype(jnp.float32)
            total = jnp.transpose(total * factor)
            if part == LAST:
                for j in range(PACK):
                    out[0, MAIN:TILE, j * FEW : (j + 1) * FEW] = total[j * REST : (j + 1) * REST]
            else:
                side = part % 2 * HALF
                out[0, block * LANES : (block + 1) * LANES, side : side + HALF] = total

    for copy in sent:
        copy.wait_send()
    others = pl.ds(0, (peers - 1) * tok)
    hand_over.wait_send()
    half_others = pl.ds(0, (lines - 1) * tok)
    if lines > 1:
        pltpu.make_async_copy(win.at[half_others], win.at[half_others], win_send.at[0]).wait()
    for message in range(len(MESSAGES)):
        sent_of = raw.at[others, size_of(message)]
        pltpu.make_async_copy(sent_of, sent_of, raw_send.at[message]).wait()


def solution(mesh):
    wide, group_len = mesh.shape["wide"], mesh.shape["chan"]
    peers = wide // SPAN
    half = SPAN * group_len // 2

    def step(activations, grads):
        tok = activations.shape[0]
        plane = peers * tok
        factor = 1.0 / math.sqrt(plane * SPAN * group_len)
        gram = pl.pallas_call(
            functools.partial(kernel, peers, group_len, factor),
            out_shape=jax.ShapeDtypeStruct((1, TILE, ROWS), jnp.float32),
            in_specs=[pl.BlockSpec(memory_space=pltpu.HBM)] * 2,
            out_specs=pl.BlockSpec(memory_space=pltpu.VMEM),
            scratch_shapes=[
                pltpu.VMEM(grads.shape, jnp.bfloat16),
                pltpu.VMEM(activations.shape, jnp.bfloat16),
                pltpu.VMEM((tok, ROWS + LANES), jnp.bfloat16),
                pltpu.VMEM((peers, tok, BLOCKS * LANES), jnp.bfloat16),
                pltpu.VMEM((plane, ROWS + LANES), jnp.bfloat16),
                pltpu.VMEM((plane, BLOCKS * LANES), jnp.bfloat16),
                pltpu.VMEM((group_len, ROWS, plane), jnp.bfloat16),
                pltpu.VMEM((2, half, BLOCK, LANES), jnp.float32),
                pltpu.VMEM((SPAN, group_len, FEW, LANES), jnp.float32),
                pltpu.VMEM((2, half, BLOCK, LANES), jnp.bfloat16),
                pltpu.VMEM((2, half, BLOCK, LANES), jnp.bfloat16),
                pltpu.SemaphoreType.DMA((2,)),
                pltpu.SemaphoreType.DMA((2,)),
                pltpu.SemaphoreType.DMA((2,)),
                pltpu.SemaphoreType.DMA((len(MESSAGES),)),
                pltpu.SemaphoreType.DMA((len(MESSAGES),)),
                pltpu.SemaphoreType.DMA((2, half, LAST + 1)),
                pltpu.SemaphoreType.DMA((2, half, LAST + 1)),
            ],
            compiler_params=pltpu.CompilerParams(
                collective_id=0, has_side_effects=True, vmem_limit_bytes=53 * 1024 * 1024
            ),
        )(activations, grads)
        return jnp.transpose(gram, (0, 2, 1))

    return jax.shard_map(
        step,
        mesh=mesh,
        in_specs=(P(("wide", "chan"), None), P(("wide", "chan"), None)),
        out_specs=P("chan", None, "wide"),
        check_vma=False,
    )
```
